128 devices in a mesh: fsdp: 4 (over x), tensor: 32 (over z, y, core).
Axes of the slice: x: 4, y: 4, z: 4, core: 2. Of those that a mesh axis runs over, the one named last changes fastest.
Arguments:
- inputs_roll: bfloat16 [1536, 4096], P('fsdp', 'tensor'), may hold values from -6 to 6
- cotangent_roll: bfloat16 [1536, 4096], P('fsdp', 'tensor'), may hold values from -0.59765625 to 0.59765625
- counts: int32 [4, 4], P('fsdp'), may hold values from 1 to 3, as said below
- w_gate: bfloat16 [4096, 16384], P('fsdp', 'tensor'), may hold values from -0.09375 to 0.09375
- w_up: bfloat16 [4096, 16384], P('fsdp', 'tensor'), may hold values from -0.09375 to 0.09375
- w_down: bfloat16 [16384, 4096], P('tensor', 'fsdp'), may hold values from -0.046875 to 0.046875
Outputs:
- grad_inputs: bfloat16 [2304, 4096], P('fsdp', 'tensor')
- grad_gate: bfloat16 [4096, 16384], P('fsdp', 'tensor')
- grad_up: bfloat16 [4096, 16384], P('fsdp', 'tensor')
- grad_down: bfloat16 [16384, 4096], P('tensor', 'fsdp')
The draws below stay inside these ranges and needn't reach their ends.
Inputs may be any that keep to these rules, and one draw needn't show every extreme that they name: Row s of counts splits rollout shard s's 8 blocks among the learner shards, in order of learner; every row sums to 8.
All inputs are finite; a program needn't handle non-finite values.
Results may differ from the reference program's by a relative error of at most 0.015.
Values may be sent and summed in bfloat16 or wider, within the bound.
A program may use at most 128 MiB of HBM per device.

```python
import jax
import jax.numpy as jnp

D = 4096
FF = 16384
BLOCK = 48
SHARE = 2
MOST = 3
KEEP = 8
ROLL_ROWS = 1536
N_FSDP = 4


def draw_counts(key, part):
    key_popular, key_jitter, key_swaps = jax.random.split(jax.random.fold_in(key, 11), 3)
    popular = jax.random.randint(key_popular, (N_FSDP,), 0, 2)
    jitter = jax.random.randint(key_jitter, (N_FSDP, N_FSDP), 0, N_FSDP)
    scores = (jitter + N_FSDP * popular[None, :]) * N_FSDP + jnp.arange(N_FSDP)[None, :]
    ranking = jnp.argsort(-scores, axis=1)
    swaps_count = jax.random.randint(key_swaps, (N_FSDP, 1), 1, N_FSDP // 2 + 1)
    positions = jnp.arange(N_FSDP)[None, :]
    amounts = SHARE + (positions < swaps_count).astype(jnp.int32) - (positions >= N_FSDP - swaps_count).astype(jnp.int32)
    sources = jnp.broadcast_to(jnp.arange(N_FSDP)[:, None], (N_FSDP, N_FSDP))
    return jnp.zeros((N_FSDP, N_FSDP), jnp.int32).at[sources, ranking].set(amounts.astype(jnp.int32))


def levels(own_key, extent, shards, smallest, top_value):
    def one(axis_at, parts):
        heights = jax.random.uniform(jax.random.fold_in(jax.random.fold_in(own_key, 6), axis_at), (parts,), jnp.float32, smallest / len(shards), top_value / len(shards))
        return jnp.repeat(jnp.exp(heights), extent[axis_at] // parts).reshape((-1,) + (1,) * (len(extent) - axis_at - 1))

    loudness = one(*shards[0])
    for cut in shards[1:]:
        loudness = loudness * one(*cut)
    return loudness


def normal_values(stream_key, dims, spread, most, shards=(), kind=jnp.bfloat16):
    values = spread * jax.random.normal(stream_key, dims, jnp.float32)
    if shards:
        values = values * levels(stream_key, dims, shards, -0.22, 0.18)
    return jnp.clip(values, -most, most).astype(kind)


def setup_inputs(seed: int = 0) -> dict:
    seeds = jax.random.split(jax.random.key(seed), 7)
    return {
        "inputs_roll": normal_values(seeds[0], (ROLL_ROWS, D), 1.0, 6.0, ((0, 4), (1, 32))),
        "cotangent_roll": normal_values(seeds[1], (ROLL_ROWS, D), 0.1, 0.59765625, ((0, 4), (1, 32))),
        "counts": draw_counts(jax.random.fold_in(seeds[6], 71), 0),
        "w_gate": normal_values(seeds[3], (D, FF), D ** -0.5, 0.09375, ((0, 4), (1, 32))),
        "w_up": normal_values(seeds[4], (D, FF), D ** -0.5, 0.09375, ((0, 4), (1, 32))),
        "w_down": normal_values(seeds[5], (FF, D), FF ** -0.5, 0.046875, ((0, 32), (1, 4))),
    }


def route_blocks(blocks, counts):
    offsets = jnp.cumsum(counts, axis=1) - counts
    slot_ids = jnp.arange(MOST, dtype=jnp.int32)
    chosen = offsets.T[:, :, None] + slot_ids[None, None, :]
    is_live = slot_ids[None, None, :] < counts.T[:, :, None]
    chosen = jnp.where(is_live, chosen, 0).astype(jnp.int32)
    sources = jnp.broadcast_to(jnp.arange(N_FSDP, dtype=jnp.int32)[None, :, None], chosen.shape)
    picked = blocks[sources, chosen]
    picked = jnp.where(is_live[:, :, :, None, None], picked, jnp.zeros_like(picked))
    return picked.reshape(N_FSDP * N_FSDP * MOST * BLOCK, blocks.shape[-1])


def reference(inputs_roll, cotangent_roll, counts, w_gate, w_up, w_down):
    features = inputs_roll.shape[1]
    inputs = route_blocks(inputs_roll.reshape(N_FSDP, KEEP, BLOCK, features), counts)
    cotangent = route_blocks(cotangent_roll.reshape(N_FSDP, KEEP, BLOCK, features), counts)
    gate_act = jnp.dot(inputs, w_gate, preferred_element_type=jnp.float32)
    up_act = jnp.dot(inputs, w_up, preferred_element_type=jnp.float32)
    sigmoid_gate = jax.nn.sigmoid(gate_act)
    silu_gate = gate_act * sigmoid_gate
    hidden = (silu_gate * up_act).astype(jnp.bfloat16)
    grad_hidden = jnp.dot(cotangent, w_down.T, preferred_element_type=jnp.float32)
    grad_gate_pre = (grad_hidden * up_act * sigmoid_gate * (1.0 + gate_act * (1.0 - sigmoid_gate))).astype(jnp.bfloat16)
    grad_up_pre = (grad_hidden * silu_gate).astype(jnp.bfloat16)
    grad_inputs = (jnp.dot(grad_gate_pre, w_gate.T, preferred_element_type=jnp.float32)
                   + jnp.dot(grad_up_pre, w_up.T, preferred_element_type=jnp.float32)).astype(jnp.bfloat16)
    grad_gate = jnp.dot(inputs.T, grad_gate_pre, preferred_element_type=jnp.float32).astype(jnp.bfloat16)
    grad_up = jnp.dot(inputs.T, grad_up_pre, preferred_element_type=jnp.float32).astype(jnp.bfloat16)
    grad_down = jnp.dot(hidden.T, cotangent, preferred_element_type=jnp.float32).astype(jnp.bfloat16)
    return (grad_inputs, grad_gate, grad_up, grad_down)
```

```python
import jax
import jax.numpy as jnp
from jax import lax
from jax.experimental import pallas as pl
from jax.experimental.pallas import tpu as pltpu
from jax.sharding import PartitionSpec as P

MESH = pl.DeviceIdType.MESH
BLOCK = 48
MOST = 3
N = 4
PARTS = 4
BF = jnp.bfloat16
F32 = jnp.float32
TALL = (((0,), (0,)), ((), ()))
WIDE = (((1,), (1,)), ((), ()))


def kernel(
    own_ref, cnt_ref, wg_ref, wu_ref, wd_ref,
    gin_ref, gg_ref, gu_ref, gd_ref,
    rows, cnts, part, r1, r2, acts, acc, q, qc, q2, zr, q3, yr, fo, fin,
    t_s, t_r, n_s, n_r, y_s, y_r, c_s, c_r, x_s, x_r, k_s, k_r, zs_s, zs_r, ys_s, ys_r, f_s, f_r,
):
    n_rows = rows.shape[4]
    x = lax.axis_index("fsdp")
    t = lax.axis_index("tensor")
    z, y, c = t // 8, (t // 2) % N, t % 2
    fb = y * 2 + c

    def ring(i, d):
        return lax.rem(i + (d + N), N)

    right, left, far = ring(x, 1), ring(x, -1), ring(x, 2)
    to_right, to_left = (right, t), (left, t)
    sibling = (x, z * 8 + y * 2 + (1 - c))

    def at_z(d):
        return (x, ring(z, d) * 8 + fb)

    def at_y(d):
        return (x, z * 8 + ring(y, d) * 2 + c)

    barrier = pltpu.get_barrier_semaphore()
    same = (x == z).astype(jnp.int32)

    def hello(device):
        pl.semaphore_signal(barrier, 1, device_id=device, device_id_type=MESH)

    for j in range(N):
        itself = (x == z) & (z == j)

        @pl.when(jnp.logical_not(itself))
        def _():
            hello((z, j * 8 + fb))
            hello((j, x * 8 + fb))

    for d in (1, 2, 3):
        hello(at_z(d))
        hello(at_y(d))
    hello(to_right)
    hello(to_left)
    hello(sibling)
    pl.semaphore_wait(barrier, 17 - 2 * same)

    pending = {}

    def send(key, src, dst, s_sem, r_sem, device):
        if key in pending:
            pending.pop(key).wait_send()
        copy = pltpu.make_async_remote_copy(
            src, dst, s_sem, r_sem, device_id=device, device_id_type=MESH
        )
        copy.start()
        pending[key] = copy
        return copy

    def arrive(dst, r_sem):
        pltpu.make_async_copy(dst, dst, r_sem).wait()

    def each_target(step):
        for j in range(N):
            itself = (x == z) & (z == j)
            step(j, itself)

    def transpose_copies(src, dst, s_sem, r_sem, start, forward=True):
        for j in range(N):
            itself = (x == z) & (z == j)
            device = (z, j * 8 + fb) if forward else (j, x * 8 + fb)
            remote = pltpu.make_async_remote_copy(
                src, dst, s_sem.at[j], r_sem, device_id=device, device_id_type=MESH
            )

            @pl.when(jnp.logical_not(itself))
            def _():
                if start:
                    remote.start()
                else:
                    remote.wait_send()

            if start:

                @pl.when(itself)
                def _():
                    pltpu.make_async_copy(src, dst, r_sem).start()

    def first_move(k, a, start):
        transpose_copies(
            own_ref.at[a, pl.ds(k * n_rows, n_rows)], rows.at[a, k, fb, x],
            t_s.at[k, a], t_r.at[k, a, x], start,
        )

    for k in range(PARTS):
        for a in range(2):
            first_move(k, a, True)
    transpose_copies(cnt_ref, cnts.at[x], n_s, n_r.at[x], True)

    def spread(k):
        for a in range(2):
            for s in range(N):
                arrive(rows.at[a, k, fb, s], t_r.at[k, a, s])
            mine = rows.at[a, k, fb]
            for d in (2, 1, 3):
                send(("y", a, d), mine, mine, y_s.at[a, d - 1], y_r.at[k, a, d - 1], at_y(d))
            send(("c", a, 0), mine, mine, c_s.at[a, 0], c_r.at[k, a, 0], sibling)

    def share(k):
        for a in range(2):
            for d in (1, 3, 2):
                theirs = rows.at[a, k, ring(y, -d) * 2 + c]
                arrive(theirs, y_r.at[k, a, d - 1])
                send(("c", a, d), theirs, theirs, c_s.at[a, d], c_r.at[k, a, d], sibling)

    def shared(k, a):
        for d in range(4):
            arrive(rows.at[a, k, ring(y, -d) * 2 + (1 - c)], c_r.at[k, a, d])

    def all_features(a, k):
        return jnp.concatenate(
            [rows[a, k, f].reshape(N * n_rows, 128) for f in range(8)], axis=1
        )

    def forward(k):
        shared(k, 0)
        lhs = all_features(0, k)
        for m, w in ((0, wg_ref), (1, wu_ref)):
            for h in range(2):
                out = jnp.dot(lhs, w[:, h * 256 : h * 256 + 256], preferred_element_type=F32)
                part[k, h, m] = out.astype(BF).reshape(N, n_rows, 256)
        shared(k, 1)
        lhs = all_features(1, k)
        for h in range(2):
            out = lax.dot_general(
                lhs, wd_ref[h * 256 : h * 256 + 256, :], WIDE, preferred_element_type=F32
            )
            part[k, h, 2] = out.astype(BF).reshape(N, n_rows, 256)
        send("s1r", part.at[k, 0, :, far], r1.at[k, 0], x_s.at[0], x_r.at[k, 0], to_right)
        send("s1l", part.at[k, 1, :, far], r1.at[k, 1], x_s.at[1], x_r.at[k, 1], to_left)

    def relay(k):
        arrive(r1.at[k, 0], x_r.at[k, 0])
        for m in range(3):
            part[k, 0, m, right] = (
                part[k, 0, m, right].astype(F32) + r1[k, 0, m].astype(F32)
            ).astype(BF)
        send("s2r", part.at[k, :, :, right], r2.at[k, 0], x_s.at[2], x_r.at[k, 2], to_right)
        arrive(r1.at[k, 1], x_r.at[k, 1])
        for m in range(3):
            part[k, 1, m, left] = (
                part[k, 1, m, left].astype(F32) + r1[k, 1, m].astype(F32)
            ).astype(BF)
        send("s2l", part.at[k, :, :, left], r2.at[k, 1], x_s.at[3], x_r.at[k, 3], to_left)

    def activate(k):
        arrive(r2.at[k, 0], x_r.at[k, 2])
        arrive(r2.at[k, 1], x_r.at[k, 3])
        for h in range(2):
            gate, up, grad_hidden = (
                part[k, h, m, x].astype(F32)
                + r2[k, 0, h, m].astype(F32)
                + r2[k, 1, h, m].astype(F32)
                for m in range(3)
            )
            sigmoid = jax.nn.sigmoid(gate)
            silu = gate * sigmoid
            acts[k, h, 0, x] = (
                grad_hidden * up * sigmoid * (1.0 + gate * (1.0 - sigmoid))
            ).astype(BF)
            acts[k, h, 1, x] = (grad_hidden * silu).astype(BF)
            acts[k, h, 2, x] = (silu * up).astype(BF)
        mine = acts.at[k, :, :, x]
        send("a1r", mine, mine, x_s.at[4], x_r.at[k, 4], to_right)
        send("a1l", mine, mine, x_s.at[5], x_r.at[k, 5], to_left)

    def pass_on(k):
        arrive(acts.at[k, :, :, left], x_r.at[k, 4])
        ref = acts.at[k, 0, :, left]
        send("a2r", ref, ref, x_s.at[6], x_r.at[k, 6], to_right)
        arrive(acts.at[k, :, :, right], x_r.at[k, 5])
        ref = acts.at[k, 1, :, right]
        send("a2l", ref, ref, x_s.at[7], x_r.at[k, 7], to_left)

    def input_terms(k):
        arrive(acts.at[k, 0, :, far], x_r.at[k, 6])
        arrive(acts.at[k, 1, :, far], x_r.at[k, 7])

        def act(m):
            return jnp.concatenate(
                [acts[k, h, m].reshape(N * n_rows, 256) for h in range(2)], axis=1
            )

        @pl.loop(0, N)
        def _(j):
            feats = pl.ds(pl.multiple_of(j * 256, 256), 256)
            out = lax.dot_general(act(0), wg_ref[feats, :], WIDE, preferred_element_type=F32)
            out += lax.dot_general(act(1), wu_ref[feats, :], WIDE, preferred_element_type=F32)
            out = out.astype(BF)
            q[k, 0, j] = out[:, :128].reshape(N, n_rows, 128)
            q[k, 1, j] = out[:, 128:].reshape(N, n_rows, 128)

        send("k", q.at[k, 1 - c], qc.at[k], k_s, k_r.at[k], sibling)

    def weight_terms(k):
        @pl.loop(0, N)
        def _(j):
            feats = pl.ds(pl.multiple_of(j * 256, 256), 256)
            lhs, cot = (
                jnp.concatenate(
                    [rows[a, k, 2 * j + i].reshape(N * n_rows, 128) for i in range(2)], axis=1
                )
                for a in range(2)
            )

            def add(i, out_ref, at, value):
                if k > 0:
                    value += acc[i, j, h]
                if k < PARTS - 1:
                    acc[i, j, h] = value
                else:
                    out_ref[at] = value.astype(BF)

            for h in range(2):
                cols = slice(h * 256, h * 256 + 256)
                for i, ref in ((0, gg_ref), (1, gu_ref)):
                    right_side = acts[k, h, i].reshape(N * n_rows, 256)
                    add(i, ref, (feats, cols), lax.dot_general(lhs, right_side, TALL, preferred_element_type=F32))
                hidden = acts[k, h, 2].reshape(N * n_rows, 256)
                add(2, gd_ref, (cols, feats), lax.dot_general(hidden, cot, TALL, preferred_element_type=F32))

    def over_cores(k):
        arrive(qc.at[k], k_r.at[k])
        for s in range(N):
            q2[k, s] = (q[k, c, :, s].astype(F32) + qc[k, :, s].astype(F32)).astype(BF)
        for d in (2, 1, 3):
            send(("z", d), q2.at[k, ring(z, d)], zr.at[k, d - 1], zs_s.at[d - 1], zs_r.at[k, d - 1], at_z(d))

    def over_z(k):
        for d in (1, 3, 2):
            arrive(zr.at[k, d - 1], zs_r.at[k, d - 1])
        q3[k] = (
            q2[k, z].astype(F32) + zr[k, 0].astype(F32) + zr[k, 1].astype(F32) + zr[k, 2].astype(F32)
        ).astype(BF)
        for d in (2, 1, 3):
            send(("yy", d), q3.at[k, ring(y, d)], yr.at[k, d - 1], ys_s.at[d - 1], ys_r.at[k, d - 1], at_y(d))

    def final_move(k, start):
        here = pl.ds(k * n_rows, n_rows)
        transpose_copies(fo.at[k], fin.at[z, here], f_s.at[k], f_r.at[k, z], start, False)

    def over_y(k):
        for d in (1, 3, 2):
            arrive(yr.at[k, d - 1], ys_r.at[k, d - 1])
        fo[k] = (
            q3[k, y].astype(F32) + yr[k, 0].astype(F32) + yr[k, 1].astype(F32) + yr[k, 2].astype(F32)
        ).astype(BF)
        final_move(k, True)

    spread(0)
    share(0)
    spread(1)
    for slot in range(PARTS + 2):
        if slot < PARTS:
            forward(slot)
        if 0 <= slot - 1 < PARTS:
            activate(slot - 1)
        if slot < PARTS:
            relay(slot)
        if slot + 1 < PARTS:
            share(slot + 1)
        if slot + 2 < PARTS:
            spread(slot + 2)
        if 0 <= slot - 1 < PARTS:
            pass_on(slot - 1)
        if 0 <= slot - 2 < PARTS:
            input_terms(slot - 2)
            weight_terms(slot - 2)
            over_cores(slot - 2)
            over_z(slot - 2)
            over_y(slot - 2)

    for s in range(N):
        arrive(cnts.at[s], n_r.at[s])
        for k in range(PARTS):
            arrive(fin.at[s, pl.ds(k * n_rows, n_rows)], f_r.at[k, s])
        lane = lax.broadcasted_iota(jnp.int32, (1, 128), 1)
        row = cnts[s, 0:1, :].astype(F32)
        offset = jnp.sum(jnp.where(lane < x, row, 0.0), axis=1, keepdims=True)
        count = jnp.sum(jnp.where(lane == x, row, 0.0), axis=1, keepdims=True)
        shape = (MOST * BLOCK, fin.shape[1])
        into = lax.broadcasted_iota(jnp.int32, shape, 0).astype(F32)
        out_of = lax.broadcasted_iota(jnp.int32, shape, 1).astype(F32)
        chosen = (out_of == offset * BLOCK + into) & (into < count * BLOCK)
        one_hot = jnp.where(chosen, 1.0, 0.0).astype(BF)
        gin_ref[s * MOST * BLOCK : (s + 1) * MOST * BLOCK, :] = jnp.dot(
            one_hot, fin[s], preferred_element_type=F32
        ).astype(BF)

    for copy in pending.values():
        copy.wait_send()
    for k in range(PARTS):
        for a in range(2):
            first_move(k, a, False)
        final_move(k, False)
    transpose_copies(cnt_ref, cnts.at[x], n_s, n_r.at[x], False)


def per_device(inputs_roll, cotangent_roll, counts, w_gate, w_up, w_down):
    height, wide = inputs_roll.shape
    n_rows = height // PARTS
    deep, hid = w_gate.shape
    own = jnp.stack([inputs_roll, cotangent_roll])
    cnt = jnp.pad(counts, ((0, 7), (0, 128 - counts.shape[1])))
    dma = pltpu.SemaphoreType.DMA
    vmem = pl.BlockSpec(memory_space=pltpu.VMEM)
    return pl.pallas_call(
        kernel,
        out_shape=(
            jax.ShapeDtypeStruct((N * MOST * BLOCK, wide), BF),
            jax.ShapeDtypeStruct((deep, hid), BF),
            jax.ShapeDtypeStruct((deep, hid), BF),
            jax.ShapeDtypeStruct((hid, deep), BF),
        ),
        in_specs=[vmem] * 5,
        out_specs=(vmem,) * 4,
        scratch_shapes=[
            pltpu.VMEM((2, PARTS, 8, N, n_rows, 128), BF),
            pltpu.VMEM((N, 8, 128), jnp.int32),
            pltpu.VMEM((PARTS, 2, 3, N, n_rows, 256), BF),
            pltpu.VMEM((PARTS, 2, 3, n_rows, 256), BF),
            pltpu.VMEM((PARTS, 2, 2, 3, n_rows, 256), BF),
            pltpu.VMEM((PARTS, 2, 3, N, n_rows, 256), BF),
            pltpu.VMEM((3, N, 2, 256, 256), F32),
            pltpu.VMEM((PARTS, 2, N, N, n_rows, 128), BF),
            pltpu.VMEM((PARTS, N, N, n_rows, 128), BF),
            pltpu.VMEM((PARTS, N, N, n_rows, 128), BF),
            pltpu.VMEM((PARTS, 3, N, n_rows, 128), BF),
            pltpu.VMEM((PARTS, N, n_rows, 128), BF),
            pltpu.VMEM((PARTS, 3, n_rows, 128), BF),
            pltpu.VMEM((PARTS, n_rows, 128), BF),
            pltpu.VMEM((N, height, 128), BF),
            dma((PARTS, 2, N)), dma((PARTS, 2, N)),
            dma((N,)), dma((N,)),
            dma((2, 3)), dma((PARTS, 2, 3)),
            dma((2, 4)), dma((PARTS, 2, 4)),
            dma((8,)), dma((PARTS, 8)),
            dma, dma((PARTS,)),
            dma((3,)), dma((PARTS, 3)),
            dma((3,)), dma((PARTS, 3)),
            dma((PARTS, N)), dma((PARTS, N)),
        ],
        compiler_params=pltpu.CompilerParams(
            collective_id=0, has_side_effects=True, vmem_limit_bytes=58 * 2**20
        ),
        name="layer",
    )(own, cnt, w_gate, w_up, w_down)


def solution(mesh):
    return jax.shard_map(
        per_device,
        mesh=mesh,
        in_specs=(
            P("fsdp", "tensor"),
            P("fsdp", "tensor"),
            P("fsdp", None),
            P("fsdp", "tensor"),
            P("fsdp", "tensor"),
            P("tensor", "fsdp"),
        ),
        out_specs=(
            P("fsdp", "tensor"),
            P("fsdp", "tensor"),
            P("fsdp", "tensor"),
            P("tensor", "fsdp"),
        ),
        check_vma=False,
    )
```

```python
import jax
import jax.numpy as jnp
from jax import lax
from jax.experimental import pallas as pl
from jax.experimental.pallas import tpu as pltpu
from jax.sharding import PartitionSpec as P

MESH = pl.DeviceIdType.MESH
BLOCK = 48
MOST = 3
N = 4
SIZES = (48, 96, 96, 96, 48)
PARTS = len(SIZES)
BF = jnp.bfloat16
F32 = jnp.float32
TALL = (((0,), (0,)), ((), ()))
WIDE = (((1,), (1,)), ((), ()))


def kernel(
    inp_ref, cot_ref, cnt_ref, wg_hbm, wu_hbm, wd_hbm,
    gin_ref, gg_ref, gu_ref, gd_ref,
    wg_ref, wu_ref, wd_ref, cnt_own,
    rows, cnts, part, r1, r2, acts, acc, q, qc, q2, zr, q3, yr, fo, fin,
    w_s, t_s, t_r, g_s, g_r, n_s, n_r, y_s, y_r, c_s, c_r, x_s, x_r, k_s, k_r, zs_s, zs_r, ys_s, ys_r, f_s, f_r,
):
    def span(k):
        return pl.ds(sum(SIZES[:k]), SIZES[k])

    loads = [
        pltpu.make_async_copy(src, dst, w_s.at[i])
        for i, (src, dst) in enumerate(((wg_hbm, wg_ref), (wu_hbm, wu_ref), (wd_hbm, wd_ref)))
    ]
    for load in loads:
        load.start()
    cnt_own[...] = jnp.zeros_like(cnt_own)
    cnt_own[0:1, 0:N] = cnt_ref[...]

    x = lax.axis_index("fsdp")
    t = lax.axis_index("tensor")
    z, y, c = t // 8, (t // 2) % N, t % 2
    fb = y * 2 + c

    def ring(i, d):
        return lax.rem(i + (d + N), N)

    right, left, far = ring(x, 1), ring(x, -1), ring(x, 2)
    to_right, to_left = (right, t), (left, t)
    mirror = (z, x * 8 + fb)
    sibling = (x, z * 8 + y * 2 + (1 - c))

    def at_x(d):
        return (ring(x, d), t)

    def at_z(d):
        return (x, ring(z, d) * 8 + fb)

    def at_y(d):
        return (x, z * 8 + ring(y, d) * 2 + c)

    barrier = pltpu.get_barrier_semaphore()
    same = (x == z).astype(jnp.int32)

    def hello(device):
        pl.semaphore_signal(barrier, 1, device_id=device, device_id_type=MESH)

    for j in range(N):

        @pl.when(jnp.logical_not((x == z) & (z == j)))
        def _():
            hello((z, j * 8 + fb))
            hello((j, x * 8 + fb))

    @pl.when(x != z)
    def _():
        hello(mirror)

    for d in (1, 2, 3):
        hello(at_x(d))
        hello(at_z(d))
        hello(at_y(d))
    hello(sibling)
    pl.semaphore_wait(barrier, 19 - 3 * same)

    pending = {}

    def send(key, src, dst, s_sem, r_sem, device):
        if key in pending:
            pending.pop(key).wait_send()
        copy = pltpu.make_async_remote_copy(
            src, dst, s_sem, r_sem, device_id=device, device_id_type=MESH
        )
        copy.start()
        pending[key] = copy
        return copy

    def arrive(dst, r_sem):
        pltpu.make_async_copy(dst, dst, r_sem).wait()

    def first_move(k, a, start):
        src, dst = (inp_ref, cot_ref)[a].at[span(k)], rows.at[a, fb, x, span(k)]
        remote = pltpu.make_async_remote_copy(
            src, dst, t_s.at[k, a], t_r.at[k, a], device_id=mirror, device_id_type=MESH
        )

        @pl.when(x != z)
        def _():
            if start:
                remote.start()
            else:
                remote.wait_send()

        if start:

            @pl.when(x == z)
            def _():
                pltpu.make_async_copy(src, dst, t_r.at[k, a]).start()

    def gather(k, a):
        mine = rows.at[a, fb, z, span(k)]
        arrive(mine, t_r.at[k, a])
        for d in (2, 1, 3):
            send(("g", a, d), mine, mine, g_s.at[a, d - 1], g_r.at[k, a, d - 1], at_z(d))

    def spread(k, a):
        for d in (1, 3, 2):
            arrive(rows.at[a, fb, ring(z, -d), span(k)], g_r.at[k, a, d - 1])
        mine = rows.at[a, fb, :, span(k)]
        for d in (2, 1, 3):
            send(("y", a, d), mine, mine, y_s.at[a, d - 1], y_r.at[k, a, d - 1], at_y(d))
        send(("c", a, 0), mine, mine, c_s.at[a, 0], c_r.at[k, a, 0], sibling)

    def share(k, a):
        for d in (1, 3, 2):
            theirs = rows.at[a, ring(y, -d) * 2 + c, :, span(k)]
            arrive(theirs, y_r.at[k, a, d - 1])
            send(("c", a, d), theirs, theirs, c_s.at[a, d], c_r.at[k, a, d], sibling)

    def shared(k, a):
        for d in range(4):
            arrive(rows.at[a, ring(y, -d) * 2 + (1 - c), :, span(k)], c_r.at[k, a, d])

    def features(a, k, blocks):
        return jnp.concatenate(
            [rows[a, f, :, span(k)].reshape(N * SIZES[k], 128) for f in blocks], axis=1
        )

    def act(m, k):
        return [acts[h, m, :, span(k)].reshape(N * SIZES[k], 256) for h in range(2)]

    def forward_a(k):
        if k == 0:
            loads[0].wait()
            loads[1].wait()
        shared(k, 0)
        lhs = features(0, k, range(8))
        for h in range(2):
            for m, w in ((0, wg_ref), (1, wu_ref)):
                out = jnp.dot(lhs, w[:, h * 256 : h * 256 + 256], preferred_element_type=F32)
                part[h, m, :, span(k)] = out.astype(BF).reshape(N, SIZES[k], 256)
            send(
                ("s1a", h), part.at[h, 0:2, far, span(k)], r1.at[h, 0:2, span(k)],
                x_s.at[h], x_r.at[k, h], (to_right, to_left)[h],
            )

    def forward_b(k):
        if k == 0:
            loads[2].wait()
        shared(k, 1)
        lhs = features(1, k, range(8))
        for h in range(2):
            out = lax.dot_general(
                lhs, wd_ref[h * 256 : h * 256 + 256, :], WIDE, preferred_element_type=F32
            )
            part[h, 2, :, span(k)] = out.astype(BF).reshape(N, SIZES[k], 256)
            send(
                ("s1b", h), part.at[h, 2, far, span(k)], r1.at[h, 2, span(k)],
                x_s.at[2 + h], x_r.at[k, 2 + h], (to_right, to_left)[h],
            )

    def relay(k):
        for h in range(2):
            near = (right, left)[h]
            arrive(r1.at[h, 0:2, span(k)], x_r.at[k, h])
            arrive(r1.at[h, 2, span(k)], x_r.at[k, 2 + h])
            for m in range(3):
                part[h, m, near, span(k)] = (
                    part[h, m, near, span(k)].astype(F32) + r1[h, m, span(k)].astype(F32)
                ).astype(BF)
            send(
                ("s2", h), part.at[:, :, near, span(k)], r2.at[h, :, :, span(k)],
                x_s.at[4 + h], x_r.at[k, 4 + h], (to_right, to_left)[h],
            )

    def activate(k):
        for h in range(2):
            arrive(r2.at[h, :, :, span(k)], x_r.at[k, 4 + h])
        for h in range(2):
            gate, up, grad_hidden = (
                part[h, m, x, span(k)].astype(F32)
                + r2[0, h, m, span(k)].astype(F32)
                + r2[1, h, m, span(k)].astype(F32)
                for m in range(3)
            )
            sigmoid = jax.nn.sigmoid(gate)
            silu = gate * sigmoid
            acts[h, 0, x, span(k)] = (
                grad_hidden * up * sigmoid * (1.0 + gate * (1.0 - sigmoid))
            ).astype(BF)
            acts[h, 1, x, span(k)] = (grad_hidden * silu).astype(BF)
            acts[h, 2, x, span(k)] = (silu * up).astype(BF)
        mine = acts.at[:, :, x, span(k)]
        for h in range(2):
            send(("a1", h), mine, mine, x_s.at[6 + h], x_r.at[k, 6 + h], (to_right, to_left)[h])

    def pass_on(k):
        for h in range(2):
            came = (left, right)[h]
            arrive(acts.at[:, :, came, span(k)], x_r.at[k, 6 + h])
            ref = acts.at[h, :, came, span(k)]
            send(("a2", h), ref, ref, x_s.at[8 + h], x_r.at[k, 8 + h], (to_right, to_left)[h])

    def input_terms(k):
        for h in range(2):
            arrive(acts.at[h, :, far, span(k)], x_r.at[k, 8 + h])

        @pl.loop(0, N)
        def _(j):
            feats = pl.ds(pl.multiple_of(j * 256, 256), 256)
            out = sum(
                lax.dot_general(
                    jnp.concatenate(act(m, k), axis=1), w[feats, :], WIDE, preferred_element_type=F32
                )
                for m, w in ((0, wg_ref), (1, wu_ref))
            ).astype(BF)
            for i in range(2):
                q[i, j, :, span(k)] = out[:, i * 128 : i * 128 + 128].reshape(N, SIZES[k], 128)

        send("k", q.at[1 - c, :, :, span(k)], qc.at[:, :, span(k)], k_s, k_r.at[k], sibling)

    def weight_terms(k):
        @pl.loop(0, N)
        def _(j):
            feats = pl.ds(pl.multiple_of(j * 256, 256), 256)
            lhs, cot = (features(a, k, (2 * j, 2 * j + 1)) for a in range(2))
            for h in range(2):
                cols = slice(h * 256, h * 256 + 256)
                for i, ref, at in ((0, gg_ref, (feats, cols)), (1, gu_ref, (feats, cols)), (2, gd_ref, (cols, feats))):
                    sides = (act(2, k)[h], cot) if i == 2 else (lhs, act(i, k)[h])
                    value = lax.dot_general(*sides, TALL, preferred_element_type=F32)
                    if k > 0:
                        value += acc[i, j, h]
                    if k < PARTS - 1:
                        acc[i, j, h] = value
                    else:
                        ref[at] = value.astype(BF)

    def over_cores(k):
        arrive(qc.at[:, :, span(k)], k_r.at[k])
        for s in range(N):
            q2[s, :, span(k)] = (q[c, :, s, span(k)].astype(F32) + qc[:, s, span(k)].astype(F32)).astype(BF)
        for d in (2, 1, 3):
            send(
                ("z", d), q2.at[ring(z, d), :, span(k)], zr.at[d - 1, :, span(k)],
                zs_s.at[d - 1], zs_r.at[k, d - 1], at_z(d),
            )

    def over_z(k):
        total = q2[z, :, span(k)].astype(F32)
        for d in (1, 3, 2):
            arrive(zr.at[d - 1, :, span(k)], zs_r.at[k, d - 1])
            total += zr[d - 1, :, span(k)].astype(F32)
        q3[:, span(k)] = total.astype(BF)
        for d in (2, 1, 3):
            send(
                ("yy", d), q3.at[ring(y, d), span(k)], yr.at[d - 1, span(k)],
                ys_s.at[d - 1], ys_r.at[k, d - 1], at_y(d),
            )

    def final_move(k, start):
        src, dst = fo.at[span(k)], fin.at[z, span(k)]
        for j in range(N):
            itself = (x == z) & (z == j)
            remote = pltpu.make_async_remote_copy(
                src, dst, f_s.at[k, j], f_r.at[k, z], device_id=(j, x * 8 + fb), device_id_type=MESH
            )

            @pl.when(jnp.logical_not(itself))
            def _():
                if start:
                    remote.start()
                else:
                    remote.wait_send()

            if start:

                @pl.when(itself)
                def _():
                    pltpu.make_async_copy(src, dst, f_r.at[k, z]).start()

    def over_y(k):
        total = q3[y, span(k)].astype(F32)
        for d in (1, 3, 2):
            arrive(yr.at[d - 1, span(k)], ys_r.at[k, d - 1])
            total += yr[d - 1, span(k)].astype(F32)
        fo[span(k)] = total.astype(BF)
        final_move(k, True)

    for k in range(PARTS):
        for a in range(2):
            first_move(k, a, True)
    cnts[x] = cnt_own[...]
    for d in (1, 2, 3):
        send(("n", d), cnt_own, cnts.at[x], n_s.at[d - 1], n_r.at[d - 1], at_x(d))

    gather(0, 0)
    gather(0, 1)
    spread(0, 0)
    spread(0, 1)
    gather(1, 0)
    gather(1, 1)
    share(0, 0)
    forward_a(0)
    share(0, 1)
    spread(1, 0)
    spread(1, 1)
    forward_b(0)
    gather(2, 0)
    gather(2, 1)
    for slot in range(PARTS + 3):
        def at(lag, *steps):
            if 0 <= slot - lag < PARTS:
                for step in steps:
                    step(slot - lag)

        if slot > 0:
            at(0, forward_a, forward_b)
        at(3, over_z)
        at(1, activate)
        at(3, over_y)
        for a in range(2):
            at(-1, lambda k: share(k, a))
        at(0, relay)
        for a in range(2):
            at(-2, lambda k: spread(k, a))
            at(-3, lambda k: gather(k, a))
        at(2, input_terms, weight_terms, over_cores)
        at(1, pass_on)

    for d in (1, 2, 3):
        arrive(cnts.at[ring(x, -d)], n_r.at[d - 1])
    for s in range(N):
        for k in range(PARTS):
            arrive(fin.at[s, span(k)], f_r.at[k, s])
        lane = lax.broadcasted_iota(jnp.int32, (1, 128), 1)
        row = cnts[s, 0:1, :].astype(F32)
        offset = jnp.sum(jnp.where(lane < x, row, 0.0), axis=1, keepdims=True)
        count = jnp.sum(jnp.where(lane == x, row, 0.0), axis=1, keepdims=True)
        shape = (MOST * BLOCK, fin.shape[1])
        into = lax.broadcasted_iota(jnp.int32, shape, 0).astype(F32)
        out_of = lax.broadcasted_iota(jnp.int32, shape, 1).astype(F32)
        chosen = (out_of == offset * BLOCK + into) & (into < count * BLOCK)
        one_hot = jnp.where(chosen, 1.0, 0.0).astype(BF)
        gin_ref[s * MOST * BLOCK : (s + 1) * MOST * BLOCK, :] = jnp.dot(
            one_hot, fin[s], preferred_element_type=F32
        ).astype(BF)

    for copy in pending.values():
        copy.wait_send()
    for k in range(PARTS):
        for a in range(2):
            first_move(k, a, False)
        final_move(k, False)


def per_device(inputs_roll, cotangent_roll, counts, w_gate, w_up, w_down):
    height, wide = inputs_roll.shape
    deep, hid = w_gate.shape
    dma = pltpu.SemaphoreType.DMA
    vmem = pl.BlockSpec(memory_space=pltpu.VMEM)
    hbm = pl.BlockSpec(memory_space=pl.ANY)
    return pl.pallas_call(
        kernel,
        out_shape=(
            pltpu.VMEM((N * MOST * BLOCK, wide), BF),
            pltpu.VMEM((deep, hid), BF),
            pltpu.VMEM((deep, hid), BF),
            pltpu.VMEM((hid, deep), BF),
        ),
        in_specs=[hbm, hbm, vmem, hbm, hbm, hbm],
        out_specs=(vmem,) * 4,
        scratch_shapes=[
            pltpu.VMEM((deep, hid), BF),
            pltpu.VMEM((deep, hid), BF),
            pltpu.VMEM((hid, deep), BF),
            pltpu.VMEM((8, 128), jnp.int32),
            pltpu.VMEM((2, 8, N, height, 128), BF),
            pltpu.VMEM((N, 8, 128), jnp.int32),
            pltpu.VMEM((2, 3, N, height, 256), BF),
            pltpu.VMEM((2, 3, height, 256), BF),
            pltpu.VMEM((2, 2, 3, height, 256), BF),
            pltpu.VMEM((2, 3, N, height, 256), BF),
            pltpu.VMEM((3, N, 2, 256, 256), F32),
            pltpu.VMEM((2, N, N, height, 128), BF),
            pltpu.VMEM((N, N, height, 128), BF),
            pltpu.VMEM((N, N, height, 128), BF),
            pltpu.VMEM((3, N, height, 128), BF),
            pltpu.VMEM((N, height, 128), BF),
            pltpu.VMEM((3, height, 128), BF),
            pltpu.VMEM((height, 128), BF),
            pltpu.VMEM((N, height, 128), BF),
            dma((3,)),
            dma((PARTS, 2)), dma((PARTS, 2)),
            dma((2, 3)), dma((PARTS, 2, 3)),
            dma((3,)), dma((3,)),
            dma((2, 3)), dma((PARTS, 2, 3)),
            dma((2, 4)), dma((PARTS, 2, 4)),
            dma((10,)), dma((PARTS, 10)),
            dma, dma((PARTS,)),
            dma((3,)), dma((PARTS, 3)),
            dma((3,)), dma((PARTS, 3)),
            dma((PARTS, N)), dma((PARTS, N)),
        ],
        compiler_params=pltpu.CompilerParams(
            collective_id=0, has_side_effects=True, vmem_limit_bytes=56 * 2**20
        ),
        name="layer",
    )(inputs_roll, cotangent_roll, counts, w_gate, w_up, w_down)


def solution(mesh):
    return jax.shard_map(
        per_device,
        mesh=mesh,
        in_specs=(
            P("fsdp", "tensor"),
            P("fsdp", "tensor"),
            P("fsdp", None),
            P("fsdp", "tensor"),
            P("fsdp", "tensor"),
            P("tensor", "fsdp"),
        ),
        out_specs=(
            P("fsdp", "tensor"),
            P("fsdp", "tensor"),
            P("fsdp", "tensor"),
            P("tensor", "fsdp"),
        ),
        check_vma=False,
    )
```

```python
import jax
import jax.numpy as jnp
from jax import lax
from jax.experimental import pallas as pl
from jax.experimental.pallas import tpu as pltpu
from jax.sharding import PartitionSpec as P

MESH = pl.DeviceIdType.MESH
BLOCK = 48
MOST = 3
N = 4
SIZES = (48, 96, 96, 96, 48)
PARTS = len(SIZES)
BF = jnp.bfloat16
F32 = jnp.float32
TALL = (((0,), (0,)), ((), ()))
WIDE = (((1,), (1,)), ((), ()))


def kernel(
    inp_ref, cot_ref, cnt_ref, wg_hbm, wu_hbm, wd_hbm,
    gin_ref, gg_ref, gu_ref, gd_ref,
    wg_ref, wu_ref, wd_ref, cnt_own,
    rows, cnts, part, r1, r2, acts, acc, q, qc, q2, zr, q3, yr, fo, fin,
    w_s, t_s, t_r, g_s, g_r, n_s, n_r, y_s, y_r, c_s, c_r, x_s, x_r, k_s, k_r, zs_s, zs_r, ys_s, ys_r, f_s, f_r,
):
    def span(k):
        return pl.ds(sum(SIZES[:k]), SIZES[k])

    loads = [
        pltpu.make_async_copy(src, dst, w_s.at[i])
        for i, (src, dst) in enumerate(((wg_hbm, wg_ref), (wu_hbm, wu_ref), (wd_hbm, wd_ref)))
    ]
    for load in loads:
        load.start()
    cnt_own[...] = jnp.zeros_like(cnt_own)
    cnt_own[0:1, 0:N] = cnt_ref[...]

    x = lax.axis_index("fsdp")
    t = lax.axis_index("tensor")
    z, y, c = t // 8, (t // 2) % N, t % 2
    fb = y * 2 + c

    def ring(i, d):
        return lax.rem(i + (d + N), N)

    right, left, far = ring(x, 1), ring(x, -1), ring(x, 2)
    to_right, to_left = (right, t), (left, t)
    mirror = (z, x * 8 + fb)
    sibling = (x, z * 8 + y * 2 + (1 - c))

    def at_x(d):
        return (ring(x, d), t)

    def at_z(d):
        return (x, ring(z, d) * 8 + fb)

    def at_y(d):
        return (x, z * 8 + ring(y, d) * 2 + c)

    barrier = pltpu.get_barrier_semaphore()
    same = (x == z).astype(jnp.int32)

    def hello(device):
        pl.semaphore_signal(barrier, 1, device_id=device, device_id_type=MESH)

    for j in range(N):

        @pl.when(jnp.logical_not((x == z) & (z == j)))
        def _():
            hello((z, j * 8 + fb))
            hello((j, x * 8 + fb))

    @pl.when(x != z)
    def _():
        hello(mirror)

    for d in (1, 2, 3):
        hello(at_x(d))
        hello(at_z(d))
        hello(at_y(d))
    hello(sibling)
    pl.semaphore_wait(barrier, 19 - 3 * same)

    pending = {}

    def send(key, src, dst, s_sem, r_sem, device):
        if key in pending:
            pending.pop(key).wait_send()
        copy = pltpu.make_async_remote_copy(
            src, dst, s_sem, r_sem, device_id=device, device_id_type=MESH
        )
        copy.start()
        pending[key] = copy
        return copy

    def arrive(dst, r_sem):
        pltpu.make_async_copy(dst, dst, r_sem).wait()

    def first_move(k, a, start):
        src, dst = (inp_ref, cot_ref)[a].at[span(k)], rows.at[a, fb, x, span(k)]
        remote = pltpu.make_async_remote_copy(
            src, dst, t_s.at[k, a], t_r.at[k, a], device_id=mirror, device_id_type=MESH
        )

        @pl.when(x != z)
        def _():
            if start:
                remote.start()
            else:
                remote.wait_send()

        if start:

            @pl.when(x == z)
            def _():
                pltpu.make_async_copy(src, dst, t_r.at[k, a]).start()

    def gather(k, a):
        mine = rows.at[a, fb, z, span(k)]
        arrive(mine, t_r.at[k, a])
        for d in (2, 1, 3):
            send(("g", a, d), mine, mine, g_s.at[a, d - 1], g_r.at[k, a, d - 1], at_z(d))

    def spread(k, a):
        for d in (1, 3, 2):
            arrive(rows.at[a, fb, ring(z, -d), span(k)], g_r.at[k, a, d - 1])
        mine = rows.at[a, fb, :, span(k)]
        for d in (2, 1, 3):
            send(("y", a, d), mine, mine, y_s.at[a, d - 1], y_r.at[k, a, d - 1], at_y(d))
        send(("c", a, 0), mine, mine, c_s.at[a, 0], c_r.at[k, a, 0], sibling)

    def share(k, a):
        for d in (1, 3, 2):
            theirs = rows.at[a, ring(y, -d) * 2 + c, :, span(k)]
            arrive(theirs, y_r.at[k, a, d - 1])
            send(("c", a, d), theirs, theirs, c_s.at[a, d], c_r.at[k, a, d], sibling)

    def shared(k, a):
        for d in range(4):
            arrive(rows.at[a, ring(y, -d) * 2 + (1 - c), :, span(k)], c_r.at[k, a, d])

    def features(a, k, blocks):
        return jnp.concatenate(
            [rows[a, f, :, span(k)].reshape(N * SIZES[k], 128) for f in blocks], axis=1
        )

    def act(m, k):
        return [acts[h, m, :, span(k)].reshape(N * SIZES[k], 256) for h in range(2)]

    def forward_a(k):
        if k == 0:
            loads[0].wait()
            loads[1].wait()
        shared(k, 0)
        lhs = features(0, k, range(8))
        for h in range(2):
            for m, w in ((0, wg_ref), (1, wu_ref)):
                out = jnp.dot(lhs, w[:, h * 256 : h * 256 + 256], preferred_element_type=F32)
                part[h, m, :, span(k)] = out.astype(BF).reshape(N, SIZES[k], 256)
            send(
                ("s1a", h), part.at[h, 0:2, far, span(k)], r1.at[h, 0:2, span(k)],
                x_s.at[h], x_r.at[k, h], (to_right, to_left)[h],
            )

    def forward_b(k):
        if k == 0:
            loads[2].wait()
        shared(k, 1)
        lhs = features(1, k, range(8))
        for h in range(2):
            out = lax.dot_general(
                lhs, wd_ref[h * 256 : h * 256 + 256, :], WIDE, preferred_element_type=F32
            )
            part[h, 2, :, span(k)] = out.astype(BF).reshape(N, SIZES[k], 256)
            send(
                ("s1b", h), part.at[h, 2, far, span(k)], r1.at[h, 2, span(k)],
                x_s.at[2 + h], x_r.at[k, 2 + h], (to_right, to_left)[h],
            )

    def relay(k):
        for h in range(2):
            near = (right, left)[h]
            arrive(r1.at[h, 0:2, span(k)], x_r.at[k, h])
            arrive(r1.at[h, 2, span(k)], x_r.at[k, 2 + h])
            for m in range(3):
                part[h, m, near, span(k)] = (
                    part[h, m, near, span(k)].astype(F32) + r1[h, m, span(k)].astype(F32)
                ).astype(BF)
            send(
                ("s2", h), part.at[:, :, near, span(k)], r2.at[h, :, :, span(k)],
                x_s.at[4 + h], x_r.at[k, 4 + h], (to_right, to_left)[h],
            )

    def activate(k):
        for h in range(2):
            arrive(r2.at[h, :, :, span(k)], x_r.at[k, 4 + h])
        for h in range(2):
            gate, up, grad_hidden = (
                part[h, m, x, span(k)].astype(F32)
                + r2[0, h, m, span(k)].astype(F32)
                + r2[1, h, m, span(k)].astype(F32)
                for m in range(3)
            )
            sigmoid = jax.nn.sigmoid(gate)
            silu = gate * sigmoid
            acts[h, 0, x, span(k)] = (
                grad_hidden * up * sigmoid * (1.0 + gate * (1.0 - sigmoid))
            ).astype(BF)
            acts[h, 1, x, span(k)] = (grad_hidden * silu).astype(BF)
            acts[h, 2, x, span(k)] = (silu * up).astype(BF)
        mine = acts.at[:, :, x, span(k)]
        for h in range(2):
            send(("a1", h), mine, mine, x_s.at[6 + h], x_r.at[k, 6 + h], (to_right, to_left)[h])

    def pass_on(k):
        for h in range(2):
            came = (left, right)[h]
            arrive(acts.at[:, :, came, span(k)], x_r.at[k, 6 + h])
            ref = acts.at[h, :, came, span(k)]
            send(("a2", h), ref, ref, x_s.at[8 + h], x_r.at[k, 8 + h], (to_right, to_left)[h])

    def input_terms(k):
        for h in range(2):
            arrive(acts.at[h, :, far, span(k)], x_r.at[k, 8 + h])

        @pl.loop(0, N)
        def _(j):
            feats = pl.ds(pl.multiple_of(j * 256, 256), 256)
            out = sum(
                lax.dot_general(
                    jnp.concatenate(act(m, k), axis=1), w[feats, :], WIDE, preferred_element_type=F32
                )
                for m, w in ((0, wg_ref), (1, wu_ref))
            ).astype(BF)
            for i in range(2):
                q[i, j, :, span(k)] = out[:, i * 128 : i * 128 + 128].reshape(N, SIZES[k], 128)

        send("k", q.at[1 - c, :, :, span(k)], qc.at[:, :, span(k)], k_s, k_r.at[k], sibling)

    def weight_terms(k):
        @pl.loop(0, N)
        def _(j):
            feats = pl.ds(pl.multiple_of(j * 256, 256), 256)
            lhs, cot = (features(a, k, (2 * j, 2 * j + 1)) for a in range(2))
            for h in range(2):
                cols = slice(h * 256, h * 256 + 256)
                for i, ref, at in ((0, gg_ref, (feats, cols)), (1, gu_ref, (feats, cols)), (2, gd_ref, (cols, feats))):
                    sides = (act(2, k)[h], cot) if i == 2 else (lhs, act(i, k)[h])
                    value = lax.dot_general(*sides, TALL, preferred_element_type=F32)
                    if k > 0:
                        value += acc[i, j, h]
                    if k < PARTS - 1:
                        acc[i, j, h] = value
                    else:
                        ref[at] = value.astype(BF)

    def over_cores(k):
        arrive(qc.at[:, :, span(k)], k_r.at[k])
        for s in range(N):
            q2[s, :, span(k)] = (q[c, :, s, span(k)].astype(F32) + qc[:, s, span(k)].astype(F32)).astype(BF)
        for d in (2, 1, 3):
            send(
                ("z", d), q2.at[ring(z, d), :, span(k)], zr.at[d - 1, :, span(k)],
                zs_s.at[d - 1], zs_r.at[k, d - 1], at_z(d),
            )

    def over_z(k):
        total = q2[z, :, span(k)].astype(F32)
        for d in (1, 3, 2):
            arrive(zr.at[d - 1, :, span(k)], zs_r.at[k, d - 1])
            total += zr[d - 1, :, span(k)].astype(F32)
        q3[:, span(k)] = total.astype(BF)
        for d in (2, 1, 3):
            send(
                ("yy", d), q3.at[ring(y, d), span(k)], yr.at[d - 1, span(k)],
                ys_s.at[d - 1], ys_r.at[k, d - 1], at_y(d),
            )

    def final_move(k, start):
        src, dst = fo.at[span(k)], fin.at[z, span(k)]
        for j in range(N):
            itself = (x == z) & (z == j)
            remote = pltpu.make_async_remote_copy(
                src, dst, f_s.at[k, j], f_r.at[k, z], device_id=(j, x * 8 + fb), device_id_type=MESH
            )

            @pl.when(jnp.logical_not(itself))
            def _():
                if start:
                    remote.start()
                else:
                    remote.wait_send()

            if start:

                @pl.when(itself)
                def _():
                    pltpu.make_async_copy(src, dst, f_r.at[k, z]).start()

    def over_y(k):
        total = q3[y, span(k)].astype(F32)
        for d in (1, 3, 2):
            arrive(yr.at[d - 1, span(k)], ys_r.at[k, d - 1])
            total += yr[d - 1, span(k)].astype(F32)
        fo[span(k)] = total.astype(BF)
        final_move(k, True)

    for k in range(PARTS):
        for a in range(2):
            first_move(k, a, True)
    cnts[x] = cnt_own[...]
    for d in (1, 2, 3):
        send(("n", d), cnt_own, cnts.at[x], n_s.at[d - 1], n_r.at[d - 1], at_x(d))

    gather(0, 0)
    gather(0, 1)
    spread(0, 0)
    spread(0, 1)
    gather(1, 0)
    gather(1, 1)
    share(0, 0)
    forward_a(0)
    share(0, 1)
    spread(1, 0)
    spread(1, 1)
    forward_b(0)
    gather(2, 0)
    gather(2, 1)
    for slot in range(PARTS + 3):
        def at(lag, *steps):
            if 0 <= slot - lag < PARTS:
                for step in steps:
                    step(slot - lag)

        if slot > 0:
            at(0, forward_a, forward_b)
        at(3, over_z)
        at(1, activate)
        at(3, over_y)
        at(0, relay)
        for a in range(2):
            at(-1, lambda k: share(k, a))
        for a in range(2):
            at(-2, lambda k: spread(k, a))
            at(-3, lambda k: gather(k, a))
        at(2, input_terms, weight_terms, over_cores)
        at(1, pass_on)

    for d in (1, 2, 3):
        arrive(cnts.at[ring(x, -d)], n_r.at[d - 1])
    for s in range(N):
        for k in range(PARTS):
            arrive(fin.at[s, span(k)], f_r.at[k, s])
        lane = lax.broadcasted_iota(jnp.int32, (1, 128), 1)
        row = cnts[s, 0:1, :].astype(F32)
        offset = jnp.sum(jnp.where(lane < x, row, 0.0), axis=1, keepdims=True)
        count = jnp.sum(jnp.where(lane == x, row, 0.0), axis=1, keepdims=True)
        shape = (MOST * BLOCK, fin.shape[1])
        into = lax.broadcasted_iota(jnp.int32, shape, 0).astype(F32)
        out_of = lax.broadcasted_iota(jnp.int32, shape, 1).astype(F32)
        chosen = (out_of == offset * BLOCK + into) & (into < count * BLOCK)
        one_hot = jnp.where(chosen, 1.0, 0.0).astype(BF)
        gin_ref[s * MOST * BLOCK : (s + 1) * MOST * BLOCK, :] = jnp.dot(
            one_hot, fin[s], preferred_element_type=F32
        ).astype(BF)

    for copy in pending.values():
        copy.wait_send()
    for k in range(PARTS):
        for a in range(2):
            first_move(k, a, False)
        final_move(k, False)


def per_device(inputs_roll, cotangent_roll, counts, w_gate, w_up, w_down):
    height, wide = inputs_roll.shape
    deep, hid = w_gate.shape
    dma = pltpu.SemaphoreType.DMA
    vmem = pl.BlockSpec(memory_space=pltpu.VMEM)
    hbm = pl.BlockSpec(memory_space=pl.ANY)
    return pl.pallas_call(
        kernel,
        out_shape=(
            pltpu.VMEM((N * MOST * BLOCK, wide), BF),
            pltpu.VMEM((deep, hid), BF),
            pltpu.VMEM((deep, hid), BF),
            pltpu.VMEM((hid, deep), BF),
        ),
        in_specs=[hbm, hbm, vmem, hbm, hbm, hbm],
        out_specs=(vmem,) * 4,
        scratch_shapes=[
            pltpu.VMEM((deep, hid), BF),
            pltpu.VMEM((deep, hid), BF),
            pltpu.VMEM((hid, deep), BF),
            pltpu.VMEM((8, 128), jnp.int32),
            pltpu.VMEM((2, 8, N, height, 128), BF),
            pltpu.VMEM((N, 8, 128), jnp.int32),
            pltpu.VMEM((2, 3, N, height, 256), BF),
            pltpu.VMEM((2, 3, height, 256), BF),
            pltpu.VMEM((2, 2, 3, height, 256), BF),
            pltpu.VMEM((2, 3, N, height, 256), BF),
            pltpu.VMEM((3, N, 2, 256, 256), F32),
            pltpu.VMEM((2, N, N, height, 128), BF),
            pltpu.VMEM((N, N, height, 128), BF),
            pltpu.VMEM((N, N, height, 128), BF),
            pltpu.VMEM((3, N, height, 128), BF),
            pltpu.VMEM((N, height, 128), BF),
            pltpu.VMEM((3, height, 128), BF),
            pltpu.VMEM((height, 128), BF),
            pltpu.VMEM((N, height, 128), BF),
            dma((3,)),
            dma((PARTS, 2)), dma((PARTS, 2)),
            dma((2, 3)), dma((PARTS, 2, 3)),
            dma((3,)), dma((3,)),
            dma((2, 3)), dma((PARTS, 2, 3)),
            dma((2, 4)), dma((PARTS, 2, 4)),
            dma((10,)), dma((PARTS, 10)),
            dma, dma((PARTS,)),
            dma((3,)), dma((PARTS, 3)),
            dma((3,)), dma((PARTS, 3)),
            dma((PARTS, N)), dma((PARTS, N)),
        ],
        compiler_params=pltpu.CompilerParams(
            collective_id=0, has_side_effects=True, vmem_limit_bytes=56 * 2**20
        ),
        name="layer",
    )(inputs_roll, cotangent_roll, counts, w_gate, w_up, w_down)


def solution(mesh):
    return jax.shard_map(
        per_device,
        mesh=mesh,
        in_specs=(
            P("fsdp", "tensor"),
            P("fsdp", "tensor"),
            P("fsdp", None),
            P("fsdp", "tensor"),
            P("fsdp", "tensor"),
            P("tensor", "fsdp"),
        ),
        out_specs=(
            P("fsdp", "tensor"),
            P("fsdp", "tensor"),
            P("fsdp", "tensor"),
            P("tensor", "fsdp"),
        ),
        check_vma=False,
    )
```
